256 devices in a mesh: prow: 16 (over y, z_hi), pcol: 16 (over x, z_lo, core).
Axes of the slice: x: 4, y: 4, z: 8 (z_hi: 4, z_lo: 2; z = z_hi * 2 + z_lo), core: 2. Of those that a mesh axis runs over, the one named last changes fastest.
Arguments:
- paper_x: bfloat16 [16384, 768], P(('prow', 'pcol')), may hold values from -6 to 6
- author_x: bfloat16 [16384, 768], P(('pcol', 'prow')), may hold values from -6 to 6
- w_self: bfloat16 [768, 768], replicated, may hold values from -0.21875 to 0.21875
- w_rel: bfloat16 [2, 768, 768], replicated, may hold values from -0.0048828125 to 0.0048828125
- w_two: bfloat16 [768, 768], replicated, may hold values from -0.0048828125 to 0.0048828125
- block_rows: int32 [16, 16, 32], P('prow', 'pcol'), may hold values from 0 to 7, as said below
- block_cols: int32 [16, 16, 32], P('prow', 'pcol'), may hold values from 0 to 7, as said below
- block_type: int32 [16, 16, 32], P('prow', 'pcol'), may hold values from 0 to 1
- block_count: int32 [16, 16], P('prow', 'pcol'), may hold values from 8 to 32, as said below
- block_vals: bfloat16 [16, 16, 32, 128, 128], P('prow', 'pcol'), may hold values from 0 to 1, as said below
Outputs:
- paper_hidden: bfloat16 [16384, 768], P(('prow', 'pcol'))
- author_out: bfloat16 [16384, 768], P(('pcol', 'prow'))
The draws below stay inside these ranges and needn't reach their ends.
Inputs may be any that keep to these rules, and one draw needn't show every extreme that they name: `block_rows`: within one tile the live and dead slots name distinct positions; block rows are below 8. `block_cols`: block columns are below 8; with block_rows, positions of one tile are distinct. `block_count`: slots 0 to count - 1 of a tile are live; some tile holds 32 live slots and some tile 32 // 4 in every draw. `block_vals`: every entry is 0 or 1.
All inputs are finite; a program needn't handle non-finite values.
Results may differ from the reference program's by a relative error of at most 0.0041.
Values may be sent and summed in bfloat16 or wider, within the bound.
No kernel may reach another device: no remote copies, remote signals or barrier semaphores. Data moves between devices by JAX's collectives and lax.ppermute only.
A program may use at most 64 MiB of HBM per device.

```python
import jax
import jax.numpy as jnp
from jax import lax

WIDTH = 768
BLOCK = 128
RELATIONS = 2
ROW_BLOCKS = 8
COL_BLOCKS = 8
SLOTS = 32
PAPERS = 16384
AUTHORS = 16384
N_PROW = 16
N_PCOL = 16


def tile_positions(key):
    keys = jax.random.split(jax.random.fold_in(key, 7), N_PROW * N_PCOL)
    chosen = jax.vmap(lambda single: jax.random.permutation(single, ROW_BLOCKS * COL_BLOCKS)[:SLOTS])(keys)
    return chosen.reshape(N_PROW, N_PCOL, SLOTS).astype(jnp.int32)


def draw_block_rows(key, part):
    return (tile_positions(key) // COL_BLOCKS).astype(jnp.int32)


def draw_block_cols(key, part):
    return (tile_positions(key) % COL_BLOCKS).astype(jnp.int32)


def draw_block_count(key, part):
    tiles = N_PROW * N_PCOL
    counts = jax.random.randint(jax.random.fold_in(key, 11), (tiles,), SLOTS // 4, SLOTS + 1)
    fullest = jax.random.randint(jax.random.fold_in(key, 12), (), 0, tiles)
    offset = jax.random.randint(jax.random.fold_in(key, 13), (), 0, tiles - 1)
    emptiest = (fullest + 1 + offset) % tiles
    places = jnp.arange(tiles, dtype=jnp.int32)
    counts = jnp.where(places == fullest, SLOTS, counts)
    counts = jnp.where(places == emptiest, SLOTS // 4, counts)
    return counts.reshape(N_PROW, N_PCOL).astype(jnp.int32)


def draw_block_vals(key, part):
    shape = (N_PROW, N_PCOL, SLOTS, BLOCK, BLOCK)
    ones = jax.random.bernoulli(jax.random.fold_in(key, 17), 0.5, shape).astype(jnp.float32)
    return ones.astype(jnp.bfloat16)


def with_ends(array, rng, least, largest):
    index_at = [jax.random.randint(jax.random.fold_in(rng, axis), (), 0, length) for axis, length in enumerate(array.shape)]
    main_axis = array.shape.index(max(array.shape))
    next_to = index_at[:main_axis] + [(index_at[main_axis] + 1) % array.shape[main_axis]] + index_at[main_axis + 1:]
    return array.at[tuple(index_at)].set(least).at[tuple(next_to)].set(largest)


def shard_levels(rng, dims, cuts, least, high):
    level = 1.0
    for position, shards_of in cuts:
        steps = jax.random.uniform(jax.random.fold_in(jax.random.fold_in(rng, 6), position), (shards_of,), jnp.float32, least / len(cuts), high / len(cuts))
        level = level * jnp.repeat(jnp.exp(steps), dims[position] // shards_of).reshape((-1,) + (1,) * (len(dims) - 1 - position))
    return level


def scatter_about(key, dims, width, most, cuts=(), kind=jnp.bfloat16):
    array = jax.random.normal(key, dims, jnp.float32) * width
    if len(cuts) > 0:
        array = shard_levels(key, dims, cuts, -0.22, 0.18) * array
    return jnp.clip(array, min=-most, max=most).astype(kind)


def setup_inputs(seed: int = 0) -> dict:
    arg_keys = jax.random.split(jax.random.key(seed), 11)
    return {
        "paper_x": scatter_about(arg_keys[0], (PAPERS, WIDTH), 1.0, 6.0, ((0, 256),)),
        "author_x": scatter_about(arg_keys[1], (AUTHORS, WIDTH), 1.0, 6.0, ((0, 256),)),
        "w_self": scatter_about(arg_keys[2], (WIDTH, WIDTH), WIDTH ** -0.5, 0.21875),
        "w_rel": scatter_about(arg_keys[3], (RELATIONS, WIDTH, WIDTH), (WIDTH * (BLOCK // 4) * SLOTS * N_PCOL // ROW_BLOCKS) ** -0.5, 0.0048828125),
        "w_two": scatter_about(arg_keys[4], (WIDTH, WIDTH), (WIDTH * (BLOCK // 4) * SLOTS * N_PROW // COL_BLOCKS) ** -0.5, 0.0048828125),
        "block_rows": draw_block_rows(jax.random.fold_in(arg_keys[10], 71), 0),
        "block_cols": draw_block_cols(jax.random.fold_in(arg_keys[10], 71), 0),
        "block_type": with_ends(jax.random.randint(arg_keys[7], (N_PROW, N_PCOL, SLOTS), 0, RELATIONS), jax.random.fold_in(arg_keys[7], 1), 0, RELATIONS - 1).astype(jnp.int32),
        "block_count": draw_block_count(jax.random.fold_in(arg_keys[10], 71), 0),
        "block_vals": draw_block_vals(jax.random.fold_in(arg_keys[10], 71), 0),
    }


def reference(paper_x, author_x, w_self, w_rel, w_two, block_rows, block_cols, block_type, block_count, block_vals):
    paper_blocks = PAPERS // BLOCK
    author_blocks = AUTHORS // BLOCK
    tiles = N_PROW * N_PCOL
    messages = jnp.stack([jnp.dot(author_x, w_rel[index], preferred_element_type=jnp.float32) for index in range(RELATIONS)]).astype(jnp.bfloat16)
    grid_row = (jnp.arange(N_PROW, dtype=jnp.int32)[:, None, None] * ROW_BLOCKS + block_rows).reshape(tiles, SLOTS).astype(jnp.int32)
    grid_col = (jnp.arange(N_PCOL, dtype=jnp.int32)[None, :, None] * COL_BLOCKS + block_cols).reshape(tiles, SLOTS).astype(jnp.int32)
    type_ids = block_type.reshape(tiles, SLOTS)
    live = (jnp.arange(SLOTS, dtype=jnp.int32)[None, None, :] < block_count[:, :, None]).astype(jnp.float32).reshape(tiles, SLOTS)
    contents = block_vals.reshape(tiles, SLOTS, BLOCK, BLOCK)
    table = messages.reshape(RELATIONS * author_blocks, BLOCK, WIDTH)

    def first_hop(total, item):
        rows_now, cols_now, types_now, mask_now, content_now = item
        picked = table[(types_now * author_blocks + cols_now).astype(jnp.int32)]
        product = jnp.einsum("kpa,kaf->kpf", content_now.astype(jnp.float32), picked.astype(jnp.float32))
        return total.at[rows_now].add(product * mask_now[:, None, None]), None

    start = jnp.zeros((paper_blocks, BLOCK, WIDTH), jnp.float32)
    gathered, _ = lax.scan(first_hop, start, (grid_row, grid_col, type_ids, live, contents))
    gathered = gathered.reshape(PAPERS, WIDTH)
    self_term = jnp.dot(paper_x, w_self, preferred_element_type=jnp.float32)
    paper_hidden = jnp.maximum(self_term + gathered, 0.0).astype(jnp.bfloat16)
    outgoing = jnp.dot(paper_hidden, w_two, preferred_element_type=jnp.float32).astype(jnp.bfloat16)
    paper_table = outgoing.reshape(paper_blocks, BLOCK, WIDTH)

    def second_hop(total, item):
        rows_now, cols_now, mask_now, content_now = item
        picked = paper_table[rows_now]
        product = jnp.einsum("kpa,kpf->kaf", content_now.astype(jnp.float32), picked.astype(jnp.float32))
        return total.at[cols_now].add(product * mask_now[:, None, None]), None

    start_two = jnp.zeros((author_blocks, BLOCK, WIDTH), jnp.float32)
    author_total, _ = lax.scan(second_hop, start_two, (grid_row, grid_col, live, contents))
    author_out = author_total.reshape(AUTHORS, WIDTH).astype(jnp.bfloat16)
    return paper_hidden, author_out
```

```python
import jax
import jax.numpy as jnp
from jax import lax
from jax.experimental import pallas as pl
from jax.experimental.pallas import tpu as pltpu
from jax.sharding import Mesh
from jax.sharding import PartitionSpec as P

PROW = ("y", "zh")
CHIPS = ("x", "zl")
F32 = jnp.float32
BF16 = jnp.bfloat16
VMEM_LIMIT = 48 * 2**20


def hop_one(rows, cols, types, count, core, x_ref, w_ref, vals_ref, keep_ref, send_ref, msgs, acc):
    relations = w_ref.shape[0]
    tile = 256
    col_blocks = acc.shape[0]
    side = acc.shape[1]
    half = side // 2

    @pl.loop(0, x_ref.shape[0] // tile)
    def _(step):
        at = pl.ds(pl.multiple_of(step * tile, tile), tile)
        x = x_ref[at, :]
        for r in range(relations):
            msgs[r, at, :] = jnp.dot(x, w_ref[r], preferred_element_type=F32).astype(BF16)

    acc[...] = jnp.zeros_like(acc)

    def slot(k, carry):
        picked = msgs[types[k], pl.ds(pl.multiple_of(cols[k] * side, side), side), :]
        acc[rows[k]] += jnp.dot(vals_ref[k], picked, preferred_element_type=F32)
        return carry

    lax.fori_loop(0, count[0], slot, 0)
    mine = pl.multiple_of(core[0] * half, half)
    other = pl.multiple_of((1 - core[0]) * half, half)

    @pl.loop(0, col_blocks)
    def _(r):
        keep_ref[r] = acc[r, pl.ds(mine, half), :].astype(BF16)
        send_ref[r] = acc[r, pl.ds(other, half), :].astype(BF16)


def hop_two(rows, cols, count, core, mine_ref, other_ref, vals_ref, out_ref, table, acc):
    row_blocks, side, _ = table.shape
    half = side // 2
    mine = pl.multiple_of(core[0] * half, half)
    other = pl.multiple_of((1 - core[0]) * half, half)

    @pl.loop(0, row_blocks)
    def _(r):
        table[r, pl.ds(mine, half), :] = mine_ref[r]
        table[r, pl.ds(other, half), :] = other_ref[r]

    acc[...] = jnp.zeros_like(acc)

    def slot(k, carry):
        acc[cols[k]] += lax.dot_general(
            vals_ref[k], table[rows[k]], (((0,), (0,)), ((), ())), preferred_element_type=F32
        )
        return carry

    lax.fori_loop(0, count[0], slot, 0)
    out_ref[...] = acc[...].astype(BF16)


def hidden_step(got_ref, self_ref, w_ref, hidden_ref, out_ref):
    total = self_ref[...]
    for i in range(got_ref.shape[0]):
        total += got_ref[i].astype(F32)
    hidden = jnp.maximum(total, 0.0).astype(BF16)
    hidden_ref[...] = hidden
    out_ref[...] = jnp.dot(hidden, w_ref[...], preferred_element_type=F32).astype(BF16)


def spec(kind):
    return pl.BlockSpec(memory_space=kind)


def call(kernel, scalars, arrays, out_shape, scratch):
    return pl.pallas_call(
        kernel,
        out_shape=out_shape,
        in_specs=[spec(pltpu.SMEM)] * len(scalars) + [spec(pltpu.VMEM)] * len(arrays),
        out_specs=jax.tree.map(lambda _: spec(pltpu.VMEM), out_shape),
        scratch_shapes=scratch,
        compiler_params=pltpu.CompilerParams(vmem_limit_bytes=VMEM_LIMIT),
    )(*scalars, *arrays)


def exchange(value):
    return lax.ppermute(value, "core", [(0, 1), (1, 0)])


def to_all(value, axes, size):
    return lax.all_to_all(jnp.broadcast_to(value[None], (size, *value.shape)), axes, 0, 0, tiled=True)


def per_device(paper_x, author_x, w_self, w_rel, w_two, block_rows, block_cols, block_type, block_count, block_vals):
    slots = block_rows.shape[2]
    side = block_vals.shape[3]
    own, width = paper_x.shape
    chips = lax.axis_size(CHIPS)
    prows = lax.axis_size(PROW)
    rows, cols, types = (a.reshape(slots) for a in (block_rows, block_cols, block_type))
    count = block_count.reshape(1)
    vals = block_vals.reshape(slots, side, side)
    core = lax.axis_index("core").astype(jnp.int32).reshape(1)
    row_blocks = chips * 2 * own // side
    col_blocks = prows * own // side

    authors = to_all(author_x, PROW, prows).reshape(prows * own, width)
    self_term = jnp.dot(paper_x, w_self, preferred_element_type=F32)
    part = jax.ShapeDtypeStruct((row_blocks, side // 2, width), BF16)
    keep, send = call(
        hop_one,
        (rows, cols, types, count, core),
        (authors, w_rel, vals),
        (part, part),
        [pltpu.VMEM((w_rel.shape[0], prows * own, width), BF16), pltpu.VMEM((row_blocks, side, width), F32)],
    )
    pair = (keep.astype(F32) + exchange(send).astype(F32)).astype(BF16)
    got = lax.all_to_all(pair, CHIPS, 0, 0, tiled=True)
    rows_out = jax.ShapeDtypeStruct((own, width), BF16)
    paper_hidden, outgoing = call(hidden_step, (), (got, self_term, w_two), (rows_out, rows_out), [])
    mine = to_all(outgoing, CHIPS, chips)
    other = exchange(mine)
    author_part = call(
        hop_two,
        (rows, cols, count, core),
        (mine, other, vals),
        jax.ShapeDtypeStruct((col_blocks, side, width), BF16),
        [pltpu.VMEM((row_blocks, side, width), BF16), pltpu.VMEM((col_blocks, side, width), F32)],
    )
    pieces = lax.all_to_all(author_part.reshape(prows, own, width), PROW, 0, 0, tiled=True)
    return paper_hidden, pieces.astype(F32).sum(0).astype(BF16)


def solution(mesh):
    split = Mesh(mesh.devices.reshape(4, 4, 4, 2, 2), (*PROW, *CHIPS, "core"))
    pcol = (*CHIPS, "core")
    tile = P(PROW, pcol)
    return jax.shard_map(
        per_device,
        mesh=split,
        in_specs=(P((*PROW, *pcol)), P((*pcol, *PROW)), P(), P(), P(), tile, tile, tile, tile, tile),
        out_specs=(P((*PROW, *pcol)), P((*pcol, *PROW))),
        check_vma=False,
    )
```

```python
import jax
import jax.numpy as jnp
from jax import lax
from jax.experimental import pallas as pl
from jax.experimental.pallas import tpu as pltpu
from jax.sharding import Mesh
from jax.sharding import PartitionSpec as P

PROW = ("y", "zh")
PCOL = ("x", "zl", "core")
F32 = jnp.float32
BF16 = jnp.bfloat16
VMEM_LIMIT = 48 * 2**20
RING = 4


def shift(value, axis, by):
    return lax.ppermute(value, axis, [(i, (i + by) % RING) for i in range(RING)])


def swap(value, axis):
    return lax.ppermute(value, axis, [(0, 1), (1, 0)])


def behind(at, by):
    return lax.rem(at + (RING - by), RING)


def build_tiles(rows, cols, types, count, place, vals_ref, one_ref, two_ref):
    y, zh, x, zl, core = (place[i] for i in range(5))
    side = vals_ref.shape[1]
    half = side // 2
    span = RING * half
    one_ref[...] = jnp.zeros_like(one_ref)
    two_ref[...] = jnp.zeros_like(two_ref)

    def slot(k, carry):
        row, col = rows[k], cols[k]
        block = vals_ref[k]
        turned = block.T
        lanes = pl.ds(pl.multiple_of(types[k] * two_ref.shape[0] + col * side, side), side)
        d = lax.rem(lax.div(row, 2) + RING - x, RING)
        e = jnp.where(lax.rem(row, 2) == zl, 0, 1)
        for c in range(2):
            at = d * span + jnp.where(core == c, 0, side) + e * half
            one_ref[pl.ds(pl.multiple_of(at, half), half), lanes] = block[c * half : (c + 1) * half]
        lanes = pl.ds(pl.multiple_of(row * side, side), side)
        d = lax.rem(lax.div(col, 2) + RING - y, RING)
        for c in range(2):
            e = lax.rem(lax.rem(col, 2) * 2 + c + RING - zh, RING)
            at = d * span + e * half
            two_ref[pl.ds(pl.multiple_of(at, half), half), lanes] = turned[c * half : (c + 1) * half]
        return carry

    lax.fori_loop(0, count[0], slot, 0)


def copy_all(pairs, sem):
    copies = [pltpu.make_async_copy(src, dst, sem.at[i]) for i, (src, dst) in enumerate(pairs)]
    for c in copies:
        c.start()
    return copies


def near_messages(*refs):
    chunks, w_ref, out_ref, table, sem = refs[:7], *refs[7:]
    own = chunks[0].shape[0]
    for c in copy_all([(chunk, table.at[pl.ds(i * own, own), :]) for i, chunk in enumerate(chunks)], sem):
        c.wait()
    for r in range(w_ref.shape[0]):
        made = jnp.dot(table[...], w_ref[r], preferred_element_type=F32).astype(BF16)
        out_ref[r] = made.reshape(out_ref.shape[1:])


def hop_one(place, *refs):
    near_ref, far, (w_ref, tile_ref, keep_ref, send_ref, table, wide_w, msgs, sem) = refs[0], refs[1:4], refs[4:]
    y, zh = place[0], place[1]
    own, width = near_ref.shape[2:]
    relations = wide_w.shape[0]
    span = RING * own
    total = msgs.shape[0] // relations
    count = RING - 1

    def chunk(r, from_y, from_z):
        return pl.ds(pl.multiple_of(r * total + (from_y * RING + from_z) * own, own), own)

    first = copy_all([(w_ref, wide_w), *((f, table.at[pl.ds(i * count, count)]) for i, f in enumerate(far))], sem)
    late = []
    for r in range(relations):
        for i in range(7):
            at = (y, behind(zh, i)) if i < RING else (behind(y, i - count), zh)
            late.append(pltpu.make_async_copy(near_ref.at[r, i], msgs.at[chunk(r, *at), :], sem.at[RING + r * 7 + i]))
    for c in late:
        c.start()
    for c in first:
        c.wait()
    for r in range(relations):
        made = jnp.dot(
            table[...].reshape(count * count * own, width), wide_w[r], preferred_element_type=F32
        ).astype(BF16)
        for d in range(1, RING):
            for e in range(1, RING):
                at = ((d - 1) * count + e - 1) * own
                msgs[chunk(r, behind(y, d), behind(zh, e)), :] = made[at : at + own]
    for c in late:
        c.wait()

    @pl.loop(0, RING)
    def _(d):
        lhs = tile_ref[pl.ds(pl.multiple_of(d * span, span), span), :]
        made = jnp.dot(lhs, msgs[...], preferred_element_type=F32).reshape(2, 2, own, width)
        keep_ref[d] = made[0]
        send_ref[d] = made[1].astype(BF16)


def hop_two(place, *refs):
    mine, other, (tile_ref, same_ref, *parts) = refs[:4], refs[4:8], refs[8:]
    wide, narrow, table, sem = parts[:3], parts[3:6], parts[6], parts[7]
    x, zl, core = (place[i] for i in range(2, 5))
    own, width = same_ref.shape[1:]
    span = RING * own
    pairs = []
    for d in range(RING):
        for e in range(2):
            block = (behind(x, d) * 2 + (zl if e == 0 else 1 - zl)) * 2
            for source, c in ((mine, core), (other, 1 - core)):
                at = pl.ds(pl.multiple_of((block + c) * own, own), own)
                pairs.append((source[d].at[e], table.at[at, :]))
    for c in copy_all(pairs, sem):
        c.wait()
    for d in range(RING):
        made = jnp.dot(tile_ref[pl.ds(d * span, span), :], table[...], preferred_element_type=F32)
        made = made.reshape(RING, own, width)
        if d == 0:
            same_ref[...] = made
        else:
            narrow[d - 1][...] = made[0].astype(BF16)
            wide[d - 1][...] = made[1:].astype(BF16)


def hidden_step(base_ref, got_ref, self_ref, w_ref, hidden_ref, out_ref):
    total = self_ref[...] + base_ref[...] + got_ref[...].astype(F32)
    hidden = jnp.maximum(total, 0.0).astype(BF16)
    hidden_ref[...] = hidden
    out_ref[...] = jnp.dot(hidden, w_ref[...], preferred_element_type=F32).astype(BF16)


def call(kernel, flops, scalars, loose, arrays, out_shape, scratch):
    def spec(kind):
        return pl.BlockSpec(memory_space=kind)

    return pl.pallas_call(
        kernel,
        out_shape=out_shape,
        in_specs=[spec(pltpu.SMEM)] * len(scalars) + [spec(pl.ANY)] * len(loose) + [spec(pltpu.VMEM)] * len(arrays),
        out_specs=jax.tree.map(lambda _: spec(pltpu.VMEM), out_shape),
        scratch_shapes=scratch,
        compiler_params=pltpu.CompilerParams(vmem_limit_bytes=VMEM_LIMIT),
        cost_estimate=pl.CostEstimate(flops=flops, bytes_accessed=4 * 2**20, transcendentals=0),
    )(*scalars, *loose, *arrays)


def total_of(parts):
    return sum(p.astype(F32) for p in parts)


def per_device(paper_x, author_x, w_self, w_rel, w_two, block_rows, block_cols, block_type, block_count, block_vals):
    slots = block_rows.shape[2]
    side = block_vals.shape[3]
    own, width = paper_x.shape
    rows, cols, types = (a.reshape(slots) for a in (block_rows, block_cols, block_type))
    count = block_count.reshape(1)
    vals = block_vals.reshape(slots, side, side)
    place = jnp.stack([lax.axis_index(a).astype(jnp.int32) for a in (*PROW, *PCOL)])
    tile_rows = 16 * own

    def shaped(*dims, dtype=BF16):
        return jax.ShapeDtypeStruct((*dims, own, width), dtype)

    relations = w_rel.shape[0]
    sems = pltpu.SemaphoreType.DMA
    tile_one, tile_two = call(
        build_tiles,
        10**9,
        (rows, cols, types, count, place),
        (),
        (vals,),
        (
            jax.ShapeDtypeStruct((tile_rows, relations * tile_rows), BF16),
            jax.ShapeDtypeStruct((tile_rows, tile_rows), BF16),
        ),
        [],
    )
    with jax.named_scope("gather_authors"):
        by_z = [shift(author_x, "zh", e) for e in range(1, RING)]
        by_y = [shift(author_x, "y", d) for d in range(1, RING)]
        by_z, by_y = lax.optimization_barrier((by_z, by_y))
        relay = jnp.stack(by_z)
        far = [shift(relay, "y", d) for d in range(1, RING)]
    near = call(
        near_messages,
        2 * relations * 7 * own * width * width,
        (),
        (author_x, *by_z, *by_y),
        (w_rel,),
        shaped(relations, 7),
        [pltpu.VMEM((7 * own, width), BF16), sems((7,))],
    )
    self_term = jnp.dot(paper_x, w_self, preferred_element_type=F32)
    keep, send = call(
        hop_one,
        2 * relations * tile_rows * tile_rows * width,
        (place,),
        (near, *far, w_rel),
        (tile_one,),
        (shaped(RING, 2, dtype=F32), shaped(RING, 2)),
        [
            pltpu.VMEM((9, own, width), BF16),
            pltpu.VMEM(w_rel.shape, BF16),
            pltpu.VMEM((relations * tile_rows, width), BF16),
            sems((RING + relations * 7,)),
        ],
    )
    with jax.named_scope("sum_papers"):
        pair = keep + swap(send, "core").astype(F32)
        by_x = [shift(pair[d].astype(BF16), "x", d) for d in range(1, RING)]
        both = total_of([pair[0], *by_x])
        last = swap(both[1].astype(BF16), "zl")
    paper_hidden, outgoing = call(
        hidden_step, 2 * own * width * width, (), (), (both[0], last, self_term, w_two), (shaped(), shaped()), []
    )
    with jax.named_scope("gather_papers"):
        near = jnp.stack([outgoing, swap(outgoing, "zl")])
        mine = [near, *(shift(near, "x", d) for d in range(1, RING))]
        other = [swap(m, "core") for m in mine]
    same, *parts = call(
        hop_two,
        2 * tile_rows * tile_rows * width,
        (place,),
        (*mine, *other),
        (tile_two,),
        (shaped(RING, dtype=F32), *[shaped(RING - 1)] * 3, *[shaped()] * 3),
        [pltpu.VMEM((tile_rows, width), BF16), sems((16,))],
    )
    with jax.named_scope("sum_authors"):
        wide = [shift(parts[d - 1], "y", d) for d in range(1, RING)]
        narrow = [shift(parts[2 + d], "y", d) for d in range(1, RING)]
        relayed = total_of([same[1:], *wide]).astype(BF16)
        by_z = [shift(relayed[e - 1], "zh", e) for e in range(1, RING)]
        author_out = total_of([same[0], *narrow, *by_z]).astype(BF16)
    return paper_hidden, author_out


def solution(mesh):
    split = Mesh(mesh.devices.reshape(4, 4, 4, 2, 2), (*PROW, *PCOL))
    tile = P(PROW, PCOL)
    return jax.shard_map(
        per_device,
        mesh=split,
        in_specs=(P((*PROW, *PCOL)), P((*PCOL, *PROW)), P(), P(), P(), tile, tile, tile, tile, tile),
        out_specs=(P((*PROW, *PCOL)), P((*PCOL, *PROW))),
        check_vma=False,
    )
```

```python
import functools

import jax
import jax.numpy as jnp
from jax import lax
from jax.experimental import pallas as pl
from jax.experimental.pallas import tpu as pltpu
from jax.sharding import Mesh
from jax.sharding import PartitionSpec as P

PROW = ("y", "zh")
PCOL = ("x", "zl", "core")
F32 = jnp.float32
BF16 = jnp.bfloat16
VMEM_LIMIT = 24 * 2**20
PLACE = 5
RING = 4


def shift(value, axis, by):
    return lax.ppermute(value, axis, [(i, (i + by) % RING) for i in range(RING)])


def swap(value, axis):
    return lax.ppermute(value, axis, [(0, 1), (1, 0)])


def behind(at, by):
    return lax.rem(at + (RING - by), RING)


def build_tiles(place, vals_ref, one_ref, two_ref, vals, sem):
    y, zh, x, zl, core = (place[i] for i in range(PLACE))
    slots, side = vals.shape[:2]
    half = side // 2
    span = RING * half
    relations = one_ref.shape[1] // two_ref.shape[1]
    load = pltpu.make_async_copy(vals_ref, vals, sem)
    load.start()
    one_ref[...] = jnp.zeros_like(one_ref)
    two_ref[...] = jnp.zeros_like(two_ref)
    load.wait()

    def slot(k, carry):
        row, col, kind = (place[PLACE + 1 + i * slots + k] for i in range(3))
        block = vals[k]
        turned = block.T
        d = lax.rem(y + RING - lax.div(col, 2), RING)
        group = jnp.where(d == 2, 3, jnp.where(d == 3, 2, d))
        at = (group * relations + kind) * span + lax.rem(col, 2) * side
        lanes = pl.ds(pl.multiple_of(at, side), side)
        d = lax.rem(lax.div(row, 2) + RING - x, RING)
        e = jnp.where(lax.rem(row, 2) == zl, 0, 1)
        for c in range(2):
            at = jnp.where(core == c, 0, RING * side) + d * side + e * half
            one_ref[pl.ds(pl.multiple_of(at, half), half), lanes] = block[c * half : (c + 1) * half]
        lanes = pl.ds(pl.multiple_of(row * side, side), side)
        d = lax.rem(lax.div(col, 2) + RING - y, RING)
        for c in range(2):
            e = lax.rem(lax.rem(col, 2) * 2 + c + RING - zh, RING)
            place_of = jnp.where(e == 2, 0, jnp.where(e == 3, 3, e + 1))
            at = d * span + place_of * half
            two_ref[pl.ds(pl.multiple_of(at, half), half), lanes] = turned[c * half : (c + 1) * half]
        return carry

    lax.fori_loop(0, place[PLACE], slot, 0)


def copy_all(pairs, sem):
    copies = [pltpu.make_async_copy(src, dst, sem.at[i]) for i, (src, dst) in enumerate(pairs)]
    for c in copies:
        c.start()
    return copies


def add_part(first, split, has_base, is_last, place, *refs):
    pieces, refs = refs[: len(split)], refs[len(split) :]
    tile_ref, w_ref = refs[:2]
    base_ref, refs = (refs[2], refs[3:]) if has_base else (None, refs[2:])
    outs, (table, msgs, tile, sem) = refs[:-4], refs[-4:]
    relations = w_ref.shape[0]
    span = tile.shape[0] // RING
    own = span // RING
    pairs = []
    for piece, chunks in zip(pieces, split, strict=True):
        for i, (group, e) in enumerate(chunks):
            at = pl.multiple_of((group * RING + behind(place[1], e)) * own, own)
            pairs.append((piece.at[pl.ds(i * own, own), :], table.at[pl.ds(at, own), :]))
    copies = copy_all([*pairs, (tile_ref.at[:, pl.ds(first * relations * span, tile.shape[1])], tile)], sem)
    for c in copies[:-1]:
        c.wait()
    for r in range(relations):
        made = jnp.dot(table[...], w_ref[r], preferred_element_type=F32).astype(BF16)
        for i in range(table.shape[0] // span):
            at = (i * relations + r) * span
            msgs[at : at + span, :] = made[i * span : (i + 1) * span]
    copies[-1].wait()
    for step in range(RING):
        at = slice(step * span, (step + 1) * span)
        made = jnp.dot(tile[at, :], msgs[...], preferred_element_type=F32)
        if has_base:
            made += base_ref[at, :]
        if is_last:
            out = outs[step // 2]
            half = step % 2 * 2
            out[half : half + 2] = made.reshape(2, *out.shape[1:]).astype(out.dtype)
        else:
            outs[0][at, :] = made


def hop_two(place, *refs):
    mine, other, refs = refs[:4], refs[4:8], refs[8:]
    tile_ref, same_ref, up_ref, down_ref, two_up_ref, two_down_ref, table, tile, sem = refs
    x, zl, core = (place[i] for i in range(2, 5))
    own, width = same_ref.shape[1:]
    span = RING * own
    pairs = [(tile_ref, tile)]
    for d in range(RING):
        for e in range(2):
            block = (behind(x, d) * 2 + (zl if e == 0 else 1 - zl)) * 2
            for source, c in ((mine, core), (other, 1 - core)):
                at = pl.ds(pl.multiple_of((block + c) * own, own), own)
                pairs.append((source[d].at[e], table.at[at, :]))
    for c in copy_all(pairs, sem):
        c.wait()
    for d in range(RING):
        made = jnp.dot(tile[pl.ds(d * span, span), :], table[...], preferred_element_type=F32)
        made = made.reshape(RING, own, width)
        if d == 2:
            two_up_ref[...] = made[:, : own // 2].astype(BF16)
            two_down_ref[...] = made[:, own // 2 :].astype(BF16)
        else:
            out = (same_ref, up_ref, None, down_ref)[d]
            out[...] = made


def hidden_step(base_ref, got_ref, w_ref, hidden_ref, out_ref):
    first = jnp.maximum(base_ref[0] + got_ref[1].astype(F32), 0.0).astype(BF16)
    second = jnp.maximum(base_ref[1] + got_ref[0].astype(F32), 0.0).astype(BF16)
    hidden_ref[...] = first
    both = jnp.concatenate([first, second])
    out_ref[...] = jnp.dot(both, w_ref[...], preferred_element_type=F32).astype(BF16).reshape(out_ref.shape)


def call(kernel, flops, scalars, loose, arrays, out_shape, scratch, loose_space=pl.ANY):
    def spec(kind):
        return pl.BlockSpec(memory_space=kind)

    return pl.pallas_call(
        kernel,
        out_shape=out_shape,
        in_specs=[spec(pltpu.SMEM)] * len(scalars) + [spec(loose_space)] * len(loose) + [spec(pltpu.VMEM)] * len(arrays),
        out_specs=jax.tree.map(lambda _: spec(pltpu.VMEM), out_shape),
        scratch_shapes=scratch,
        compiler_params=pltpu.CompilerParams(vmem_limit_bytes=VMEM_LIMIT),
        cost_estimate=pl.CostEstimate(flops=flops, bytes_accessed=4 * 2**20, transcendentals=0),
    )(*scalars, *loose, *arrays)


def total_of(parts):
    return sum(p.astype(F32) for p in parts)


def per_device(paper_x, author_x, w_self, w_rel, w_two, block_rows, block_cols, block_type, block_count, block_vals):
    slots = block_rows.shape[2]
    side = block_vals.shape[3]
    own, width = paper_x.shape
    vals = block_vals.reshape(slots, side, side)
    at = jnp.stack([lax.axis_index(a).astype(jnp.int32) for a in (*PROW, *PCOL)])
    place = jnp.concatenate([at, *(a.reshape(-1) for a in (block_count, block_rows, block_cols, block_type))])
    tile_rows = 16 * own

    def shaped(*dims, dtype=BF16):
        return jax.ShapeDtypeStruct((*dims, own, width), dtype)

    relations = w_rel.shape[0]
    sems = pltpu.SemaphoreType.DMA
    tile_one, tile_two = call(
        build_tiles,
        10**9,
        (place,),
        (vals,),
        (),
        (
            jax.ShapeDtypeStruct((tile_rows, relations * tile_rows), BF16),
            jax.ShapeDtypeStruct((tile_rows, tile_rows), BF16),
        ),
        [pltpu.VMEM(vals.shape, BF16), sems(())],
        pltpu.HBM,
    )
    self_term = jnp.dot(paper_x, w_self, preferred_element_type=F32)
    span = RING * own

    def part(first, groups, split, pieces, base, out_shape):
        return call(
            functools.partial(add_part, first, split, base is not None, first + groups == RING),
            10**9,
            (place,),
            (*pieces, tile_one),
            (w_rel,) if base is None else (w_rel, base),
            out_shape,
            [
                pltpu.VMEM((groups * span, width), BF16),
                pltpu.VMEM((groups * relations * span, width), BF16),
                pltpu.VMEM((tile_rows, groups * relations * span), BF16),
                sems((RING * groups + 1,)),
            ],
        )

    base_shape = jax.ShapeDtypeStruct((tile_rows, width), F32)
    with jax.named_scope("gather_authors"):
        by_z = [shift(author_x, "zh", e) for e in range(1, RING)]
        by_z, tile_one, tile_two = lax.optimization_barrier((by_z, tile_one, tile_two))
        relay = jnp.concatenate([author_x, *by_z])
        ups, downs = shift(relay, "y", 1), shift(relay, "y", RING - 1)
    base = part(0, 1, [[(0, e)] for e in range(RING)], (author_x, *by_z), None, base_shape)
    with jax.named_scope("forward_authors"):
        ups, downs, base = lax.optimization_barrier((ups, downs, base))
        up_two = shift(ups[: 2 * own], "y", 1)
        down_two = shift(downs[2 * own :], "y", RING - 1)
    base = part(1, 2, [[(g, e) for e in range(RING)] for g in range(2)], (ups, downs), base, base_shape)
    keep, send = part(
        3,
        1,
        [[(0, 0), (0, 1)], [(0, 2), (0, 3)]],
        (up_two, down_two),
        base,
        (shaped(RING, 2, dtype=F32), shaped(RING, 2)),
    )
    with jax.named_scope("sum_papers"):
        pair = keep + swap(send, "core").astype(F32)
        by_x = [shift(pair[d].astype(BF16), "x", d) for d in range(1, RING)]
        both = total_of([pair[0], *by_x])
        both = jnp.stack([both[0] + self_term, both[1]])
        got = swap(both.astype(BF16), "zl")
    paper_hidden, outgoing = call(
        hidden_step, 4 * own * width * width, (), (), (both, got, w_two), (shaped(), shaped(2)), []
    )
    with jax.named_scope("gather_papers"):
        mine = [outgoing, *(shift(outgoing, "x", d) for d in range(1, RING))]
        other = [swap(m, "core") for m in mine]
    whole = shaped(RING, dtype=F32)
    piece = jax.ShapeDtypeStruct((RING, own // 2, width), BF16)
    same, up, down, two_up, two_down = call(
        hop_two,
        10**9,
        (place,),
        (*mine, *other, tile_two),
        (),
        (whole, whole, whole, piece, piece),
        [pltpu.VMEM((tile_rows, width), BF16), pltpu.VMEM((tile_rows, tile_rows), BF16), sems((17,))],
    )
    with jax.named_scope("sum_authors"):
        half = own // 2
        from_down = shift(two_up, "y", 1).astype(F32)
        from_up = shift(two_down, "y", RING - 1).astype(F32)
        up = jnp.concatenate([up[:, :half] + from_down, up[:, half:]], axis=1).astype(BF16)
        down = jnp.concatenate([down[:, :half], down[:, half:] + from_up], axis=1).astype(BF16)
        opposite = total_of([same[0], shift(up[0], "y", 1), shift(down[0], "y", RING - 1)])
        rest = total_of([same[1:], shift(up[1:], "y", 1), shift(down[1:], "y", RING - 1)])
        by_z = [
            shift(opposite.astype(BF16), "zh", 2),
            shift(rest[1].astype(BF16), "zh", 1),
            shift(rest[2].astype(BF16), "zh", RING - 1),
        ]
        author_out = total_of([rest[0], *by_z]).astype(BF16)
    return paper_hidden, author_out


def solution(mesh):
    split = Mesh(mesh.devices.reshape(4, 4, 4, 2, 2), (*PROW, *PCOL))
    tile = P(PROW, PCOL)
    return jax.shard_map(
        per_device,
        mesh=split,
        in_specs=(P((*PROW, *PCOL)), P((*PCOL, *PROW)), P(), P(), P(), tile, tile, tile, tile, tile),
        out_specs=(P((*PROW, *PCOL)), P((*PCOL, *PROW))),
        check_vma=False,
    )
```

```python
import functools

import jax
import jax.numpy as jnp
from jax import lax
from jax.experimental import pallas as pl
from jax.experimental.pallas import tpu as pltpu
from jax.sharding import Mesh
from jax.sharding import PartitionSpec as P

PROW = ("y", "zh")
PCOL = ("x", "zl", "core")
F32 = jnp.float32
BF16 = jnp.bfloat16
VMEM_LIMIT = 24 * 2**20
PLACE = 5
RING = 4


def shift(value, axis, by):
    return lax.ppermute(value, axis, [(i, (i + by) % RING) for i in range(RING)])


def swap(value, axis):
    return lax.ppermute(value, axis, [(0, 1), (1, 0)])


def behind(at, by):
    return lax.rem(at + (RING - by), RING)


def build_tiles(place, vals, one_ref, two_ref):
    y, zh, x, zl, core = (place[i] for i in range(PLACE))
    slots, side = vals.shape[:2]
    half = side // 2
    span = RING * half
    relations = one_ref.shape[1] // two_ref.shape[1]
    one_ref[...] = jnp.zeros_like(one_ref)
    two_ref[...] = jnp.zeros_like(two_ref)

    def slot(k, carry):
        row, col, kind = (place[PLACE + 1 + i * slots + k] for i in range(3))
        block = [vals[k, pl.ds(pl.multiple_of(c * half, half), half), :] for c in (core, 1 - core)]
        turned = jnp.concatenate(block).T
        d = lax.rem(y + RING - lax.div(col, 2), RING)
        group = jnp.where(d == 2, 3, jnp.where(d == 3, 2, d))
        at = (group * relations + kind) * span + lax.rem(col, 2) * side
        lanes = pl.ds(pl.multiple_of(at, side), side)
        d = lax.rem(lax.div(row, 2) + RING - x, RING)
        e = jnp.where(lax.rem(row, 2) == zl, 0, 1)
        for c in range(2):
            at = (c * RING + d) * side + e * half
            one_ref[pl.ds(pl.multiple_of(at, half), half), lanes] = block[c]
        d = lax.rem(x + RING - lax.div(row, 2), RING)
        lanes = pl.ds(pl.multiple_of((d * 2 + e) * side, side), side)
        d = lax.rem(lax.div(col, 2) + RING - y, RING)
        for c in range(2):
            e = lax.rem(lax.rem(col, 2) * 2 + c + RING - zh, RING)
            place_of = jnp.where(e == 2, 0, jnp.where(e == 3, 3, e + 1))
            at = d * span + place_of * half
            two_ref[pl.ds(pl.multiple_of(at, half), half), lanes] = turned[c * half : (c + 1) * half]
        return carry

    lax.fori_loop(0, place[PLACE], slot, 0)


def add_product(step, first, tile_ref, msgs_ref, base_ref):
    span = tile_ref.shape[0] // RING
    at = slice(step * span, (step + 1) * span)
    made = jnp.dot(tile_ref[at, first : first + msgs_ref.shape[0]], msgs_ref[...], preferred_element_type=F32)
    return made if base_ref is None else made + base_ref[at, :]


def add_part(first, split, has_base, is_last, place, *refs):
    tile_ref, w_ref, refs = refs[0], refs[1], refs[2:]
    base_ref, refs = (refs[0], refs[1:]) if has_base else (None, refs)
    pieces, (out_ref, msgs, table) = refs[: len(split)], refs[len(split) :]
    relations = w_ref.shape[0]
    span = tile_ref.shape[0] // RING
    own = span // RING
    for piece, chunks in zip(pieces, split, strict=True):
        for i, (group, e) in enumerate(chunks):
            at = pl.multiple_of((group * RING + behind(place[1], e)) * own, own)
            table[pl.ds(at, own), :] = piece[i * own : (i + 1) * own, :]
    for r in range(relations):
        made = jnp.dot(table[...], w_ref[r], preferred_element_type=F32).astype(BF16)
        for i in range(table.shape[0] // span):
            at = (i * relations + r) * span
            msgs[at : at + span, :] = made[i * span : (i + 1) * span]
    skip = first * relations * span
    if is_last:
        for step in range(2):
            made = add_product(2 + step, skip, tile_ref, msgs, base_ref)
            out_ref[2 * step : 2 * step + 2] = made.reshape(2, *out_ref.shape[1:]).astype(BF16)
    else:
        for step in range(RING):
            out_ref[step * span : (step + 1) * span, :] = add_product(step, skip, tile_ref, msgs, base_ref)


def keep_part(msgs_ref, tile_ref, base_ref, out_ref):
    skip = tile_ref.shape[1] - msgs_ref.shape[0]
    for step in range(2):
        made = add_product(step, skip, tile_ref, msgs_ref, base_ref)
        out_ref[2 * step : 2 * step + 2] = made.reshape(2, *out_ref.shape[1:])


def hop_two(*refs):
    mine, other, refs = refs[:4], refs[4:8], refs[8:]
    tile_ref, same_ref, up_ref, down_ref, two_up_ref, two_down_ref, table = refs
    own, width = same_ref.shape[1:]
    span = RING * own
    for d in range(RING):
        for e in range(2):
            at = (d * 2 + e) * 2 * own
            table[at : at + own, :] = mine[d][e]
            table[at + own : at + 2 * own, :] = other[d][e]
    for d in range(RING):
        made = jnp.dot(tile_ref[d * span : (d + 1) * span, :], table[...], preferred_element_type=F32)
        made = made.reshape(RING, own, width)
        if d == 2:
            two_up_ref[...] = made[:, : own // 2].astype(BF16)
            two_down_ref[...] = made[:, own // 2 :].astype(BF16)
        else:
            out = (same_ref, up_ref, None, down_ref)[d]
            out[...] = made


def hidden_step(base_ref, got_ref, w_ref, hidden_ref, out_ref):
    first = jnp.maximum(base_ref[0] + got_ref[1].astype(F32), 0.0).astype(BF16)
    second = jnp.maximum(base_ref[1] + got_ref[0].astype(F32), 0.0).astype(BF16)
    hidden_ref[...] = first
    both = jnp.concatenate([first, second])
    out_ref[...] = jnp.dot(both, w_ref[...], preferred_element_type=F32).astype(BF16).reshape(out_ref.shape)


def call(kernel, flops, scalars, arrays, out_shape, scratch):
    def spec(kind):
        return pl.BlockSpec(memory_space=kind)

    return pl.pallas_call(
        kernel,
        out_shape=out_shape,
        in_specs=[spec(pltpu.SMEM)] * len(scalars) + [spec(pltpu.VMEM)] * len(arrays),
        out_specs=jax.tree.map(lambda _: spec(pltpu.VMEM), out_shape),
        scratch_shapes=scratch,
        compiler_params=pltpu.CompilerParams(vmem_limit_bytes=VMEM_LIMIT),
        cost_estimate=pl.CostEstimate(flops=flops, bytes_accessed=4 * 2**20, transcendentals=0),
    )(*scalars, *arrays)


def total_of(parts):
    return sum(p.astype(F32) for p in parts)


def per_device(paper_x, author_x, w_self, w_rel, w_two, block_rows, block_cols, block_type, block_count, block_vals):
    slots = block_rows.shape[2]
    side = block_vals.shape[3]
    own, width = paper_x.shape
    vals = block_vals.reshape(slots, side, side)
    at = jnp.stack([lax.axis_index(a).astype(jnp.int32) for a in (*PROW, *PCOL)])
    place = jnp.concatenate([at, *(a.reshape(-1) for a in (block_count, block_rows, block_cols, block_type))])
    tile_rows = 16 * own

    def shaped(*dims, dtype=BF16):
        return jax.ShapeDtypeStruct((*dims, own, width), dtype)

    relations = w_rel.shape[0]
    tile_one, tile_two = call(
        build_tiles,
        10**9,
        (place,),
        (vals,),
        (
            jax.ShapeDtypeStruct((tile_rows, relations * tile_rows), BF16),
            jax.ShapeDtypeStruct((tile_rows, tile_rows), BF16),
        ),
        [],
    )
    self_term = jnp.dot(paper_x, w_self, preferred_element_type=F32)
    span = RING * own

    def part(first, groups, split, pieces, base, out_shape):
        is_last = first + groups == RING
        rows = groups * relations * span
        table = pltpu.VMEM((groups * span, width), BF16)
        return call(
            functools.partial(add_part, first, split, base is not None, is_last),
            10**9,
            (place,),
            (tile_one, w_rel, *pieces) if base is None else (tile_one, w_rel, base, *pieces),
            (out_shape, jax.ShapeDtypeStruct((rows, width), BF16)) if is_last else out_shape,
            [table] if is_last else [pltpu.VMEM((rows, width), BF16), table],
        )

    base_shape = jax.ShapeDtypeStruct((tile_rows, width), F32)
    with jax.named_scope("gather_authors"):
        by_z = [shift(author_x, "zh", e) for e in range(1, RING)]
        by_z, tile_one, tile_two = lax.optimization_barrier((by_z, tile_one, tile_two))
        own_up, own_down = shift(author_x, "y", 1), shift(author_x, "y", RING - 1)
        by_z, own_up, own_down = lax.optimization_barrier((by_z, own_up, own_down))
        relay = jnp.concatenate(by_z)
        ups, downs = shift(relay, "y", 1), shift(relay, "y", RING - 1)
    base = part(0, 1, [[(0, e)] for e in range(RING)], (author_x, *by_z), None, base_shape)
    with jax.named_scope("forward_authors"):
        ups, downs, base, self_term = lax.optimization_barrier((ups, downs, base, self_term))
        up_two = shift(jnp.concatenate([own_up, ups[:own]]), "y", 1)
        down_two = shift(downs[own:], "y", RING - 1)
    split = [es for g in range(2) for es in ([(g, 0)], [(g, e) for e in range(1, RING)])]
    base = part(1, 2, split, (own_up, ups, own_down, downs), base, base_shape)
    send, msgs = part(
        3,
        1,
        [[(0, 0), (0, 1)], [(0, 2), (0, 3)]],
        (up_two, down_two),
        base,
        shaped(RING, 2),
    )
    keep = call(keep_part, 10**9, (), (msgs, tile_one, base), shaped(RING, 2, dtype=F32), [])
    with jax.named_scope("sum_papers"):
        pair = keep + swap(send, "core").astype(F32)
        by_x = [shift(pair[d].astype(BF16), "x", d) for d in range(1, RING)]
        both = total_of([pair[0], *by_x])
        both = jnp.stack([both[0] + self_term, both[1]])
        got = swap(both.astype(BF16), "zl")
    paper_hidden, outgoing = call(
        hidden_step, 4 * own * width * width, (), (both, got, w_two), (shaped(), shaped(2)), []
    )
    with jax.named_scope("gather_papers"):
        mine = [outgoing, *(shift(outgoing, "x", d) for d in range(1, RING))]
        other = [swap(m, "core") for m in mine]
    whole = shaped(RING, dtype=F32)
    piece = jax.ShapeDtypeStruct((RING, own // 2, width), BF16)
    same, up, down, two_up, two_down = call(
        hop_two,
        10**9,
        (),
        (*mine, *other, tile_two),
        (whole, whole, whole, piece, piece),
        [pltpu.VMEM((tile_rows, width), BF16)],
    )
    with jax.named_scope("sum_authors"):
        half = own // 2
        from_down = shift(two_up, "y", 1).astype(F32)
        from_up = shift(two_down, "y", RING - 1).astype(F32)
        up = jnp.concatenate([up[:, :half] + from_down, up[:, half:]], axis=1).astype(BF16)
        down = jnp.concatenate([down[:, :half], down[:, half:] + from_up], axis=1).astype(BF16)
        opposite = total_of([same[0], shift(up[0], "y", 1), shift(down[0], "y", RING - 1)])
        rest = total_of([same[1:], shift(up[1:], "y", 1), shift(down[1:], "y", RING - 1)])
        by_z = [
            shift(opposite.astype(BF16), "zh", 2),
            shift(rest[1].astype(BF16), "zh", 1),
            shift(rest[2].astype(BF16), "zh", RING - 1),
        ]
        author_out = total_of([rest[0], *by_z]).astype(BF16)
    return paper_hidden, author_out


def solution(mesh):
    split = Mesh(mesh.devices.reshape(4, 4, 4, 2, 2), (*PROW, *PCOL))
    tile = P(PROW, PCOL)
    return jax.shard_map(
        per_device,
        mesh=split,
        in_specs=(P((*PROW, *PCOL)), P((*PCOL, *PROW)), P(), P(), P(), tile, tile, tile, tile, tile),
        out_specs=(P((*PROW, *PCOL)), P((*PCOL, *PROW))),
        check_vma=False,
    )
```

```python
import functools

import jax
import jax.numpy as jnp
from jax import lax
from jax.experimental import pallas as pl
from jax.experimental.pallas import tpu as pltpu
from jax.sharding import Mesh
from jax.sharding import PartitionSpec as P

PROW = ("y", "zh")
PCOL = ("x", "zl", "core")
F32 = jnp.float32
BF16 = jnp.bfloat16
VMEM_LIMIT = 24 * 2**20
PLACE = 5
RING = 4


def shift(value, axis, by):
    return lax.ppermute(value, axis, [(i, (i + by) % RING) for i in range(RING)])


def swap(value, axis):
    return lax.ppermute(value, axis, [(0, 1), (1, 0)])


def behind(at, by):
    return lax.rem(at + (RING - by), RING)


def build_one(place, vals, one_ref):
    y, _, x, zl, core = (place[i] for i in range(PLACE))
    slots, side = vals.shape[:2]
    half = side // 2
    span = RING * half
    relations = one_ref.shape[1] // one_ref.shape[0]
    one_ref[...] = jnp.zeros_like(one_ref)

    def slot(k, carry):
        row, col, kind = (place[PLACE + 1 + i * slots + k] for i in range(3))
        d = lax.rem(y + RING - lax.div(col, 2), RING)
        group = jnp.where(d == 2, 3, jnp.where(d == 3, 2, d))
        at = (group * relations + kind) * span + lax.rem(col, 2) * side
        lanes = pl.ds(pl.multiple_of(at, side), side)
        d = lax.rem(lax.div(row, 2) + RING - x, RING)
        e = jnp.where(lax.rem(row, 2) == zl, 0, 1)
        for i, c in enumerate((core, 1 - core)):
            at = (i * RING + d) * side + e * half
            block = vals[k, pl.ds(pl.multiple_of(c * half, half), half), :]
            one_ref[pl.ds(pl.multiple_of(at, half), half), lanes] = block
        return carry

    lax.fori_loop(0, place[PLACE], slot, 0)


def build_two(place, vals, two_ref):
    y, zh, x, zl, core = (place[i] for i in range(PLACE))
    slots, side = vals.shape[:2]
    half = side // 2
    two_ref[...] = jnp.zeros_like(two_ref)

    def slot(k, carry):
        row, col = (place[PLACE + 1 + i * slots + k] for i in range(2))
        block = [vals[k, pl.ds(pl.multiple_of(c * half, half), half), :] for c in (core, 1 - core)]
        turned = jnp.concatenate(block).T
        d = lax.rem(x + RING - lax.div(row, 2), RING)
        e = jnp.where(lax.rem(row, 2) == zl, 0, 1)
        lanes = pl.ds(pl.multiple_of((d * 2 + e) * side, side), side)
        d = lax.rem(lax.div(col, 2) + RING - y, RING)
        for c in range(2):
            e = lax.rem(lax.rem(col, 2) * 2 + c + RING - zh, RING)
            place_of = jnp.where(e == 2, 0, jnp.where(e == 3, 3, e + 1))
            at = (d * RING + place_of) * half
            two_ref[pl.ds(pl.multiple_of(at, half), half), lanes] = turned[c * half : (c + 1) * half]
        return carry

    lax.fori_loop(0, place[PLACE], slot, 0)


def add_product(step, first, tile_ref, msgs_ref, base_ref):
    span = tile_ref.shape[0] // RING
    at = slice(step * span, (step + 1) * span)
    made = jnp.dot(tile_ref[at, first : first + msgs_ref.shape[0]], msgs_ref[...], preferred_element_type=F32)
    return made if base_ref is None else made + base_ref[at, :]


def add_part(first, split, has_base, is_last, place, *refs):
    tile_ref, w_ref, refs = refs[0], refs[1], refs[2:]
    base_ref, refs = (refs[0], refs[1:]) if has_base else (None, refs)
    pieces, (out_ref, msgs, table) = refs[: len(split)], refs[len(split) :]
    relations = w_ref.shape[0]
    span = tile_ref.shape[0] // RING
    own = span // RING
    for piece, chunks in zip(pieces, split, strict=True):
        for i, (group, e) in enumerate(chunks):
            at = pl.multiple_of((group * RING + behind(place[1], e)) * own, own)
            table[pl.ds(at, own), :] = piece[i * own : (i + 1) * own, :]
    for r in range(relations):
        made = jnp.dot(table[...], w_ref[r], preferred_element_type=F32).astype(BF16)
        for i in range(table.shape[0] // span):
            at = (i * relations + r) * span
            msgs[at : at + span, :] = made[i * span : (i + 1) * span]
    skip = first * relations * span
    if is_last:
        for step in range(2):
            made = add_product(2 + step, skip, tile_ref, msgs, base_ref)
            out_ref[2 * step : 2 * step + 2] = made.reshape(2, *out_ref.shape[1:]).astype(BF16)
    else:
        for step in range(RING):
            out_ref[step * span : (step + 1) * span, :] = add_product(step, skip, tile_ref, msgs, base_ref)


def keep_part(msgs_ref, tile_ref, base_ref, out_ref):
    skip = tile_ref.shape[1] - msgs_ref.shape[0]
    for step in range(2):
        made = add_product(step, skip, tile_ref, msgs_ref, base_ref)
        out_ref[2 * step : 2 * step + 2] = made.reshape(2, *out_ref.shape[1:])


def hop_two_first(*refs):
    mine, other, (tile_ref, two_up_ref, two_down_ref, table_ref) = refs[:RING], refs[RING : 2 * RING], refs[2 * RING :]
    own = two_up_ref.shape[1] * 2
    for d in range(RING):
        for e in range(2):
            at = (d * 2 + e) * 2 * own
            table_ref[at : at + own, :] = mine[d][e]
            table_ref[at + own : at + 2 * own, :] = other[d][e]
    span = RING * own
    made = jnp.dot(tile_ref[2 * span : 3 * span, :], table_ref[...], preferred_element_type=F32)
    made = made.astype(BF16).reshape(RING, own, table_ref.shape[1])
    two_up_ref[...] = made[:, : own // 2]
    two_down_ref[...] = made[:, own // 2 :]


def hop_two_rest(table_ref, tile_ref, same_ref, up_ref, down_ref):
    span = same_ref.shape[0] * same_ref.shape[1]
    for d, out in ((1, up_ref), (3, down_ref), (0, same_ref)):
        made = jnp.dot(tile_ref[d * span : (d + 1) * span, :], table_ref[...], preferred_element_type=F32)
        out[...] = made.reshape(out.shape)


def hidden_step(base_ref, got_ref, w_ref, hidden_ref, out_ref):
    first = jnp.maximum(base_ref[0] + got_ref[1].astype(F32), 0.0).astype(BF16)
    second = jnp.maximum(base_ref[1] + got_ref[0].astype(F32), 0.0).astype(BF16)
    hidden_ref[...] = first
    both = jnp.concatenate([first, second])
    out_ref[...] = jnp.dot(both, w_ref[...], preferred_element_type=F32).astype(BF16).reshape(out_ref.shape)


def call(kernel, flops, scalars, arrays, out_shape, scratch):
    def spec(kind):
        return pl.BlockSpec(memory_space=kind)

    return pl.pallas_call(
        kernel,
        out_shape=out_shape,
        in_specs=[spec(pltpu.SMEM)] * len(scalars) + [spec(pltpu.VMEM)] * len(arrays),
        out_specs=jax.tree.map(lambda _: spec(pltpu.VMEM), out_shape),
        scratch_shapes=scratch,
        compiler_params=pltpu.CompilerParams(vmem_limit_bytes=VMEM_LIMIT),
        cost_estimate=pl.CostEstimate(flops=flops, bytes_accessed=4 * 2**20, transcendentals=0),
    )(*scalars, *arrays)


def total_of(parts):
    return sum(p.astype(F32) for p in parts)


def per_device(paper_x, author_x, w_self, w_rel, w_two, block_rows, block_cols, block_type, block_count, block_vals):
    slots = block_rows.shape[2]
    side = block_vals.shape[3]
    own, width = paper_x.shape
    vals = block_vals.reshape(slots, side, side)
    at = jnp.stack([lax.axis_index(a).astype(jnp.int32) for a in (*PROW, *PCOL)])
    place = jnp.concatenate([at, *(a.reshape(-1) for a in (block_count, block_rows, block_cols, block_type))])
    tile_rows = 16 * own

    def shaped(*dims, dtype=BF16):
        return jax.ShapeDtypeStruct((*dims, own, width), dtype)

    relations = w_rel.shape[0]
    tile = jax.ShapeDtypeStruct((tile_rows, relations * tile_rows), BF16)
    tile_one = call(build_one, 10**9, (place,), (vals,), tile, [])
    self_term = jnp.dot(paper_x, w_self, preferred_element_type=F32)
    span = RING * own

    def part(first, groups, split, pieces, base, out_shape):
        is_last = first + groups == RING
        rows = groups * relations * span
        table = pltpu.VMEM((groups * span, width), BF16)
        return call(
            functools.partial(add_part, first, split, base is not None, is_last),
            10**9,
            (place,),
            (tile_one, w_rel, *pieces) if base is None else (tile_one, w_rel, base, *pieces),
            (out_shape, jax.ShapeDtypeStruct((rows, width), BF16)) if is_last else out_shape,
            [table] if is_last else [pltpu.VMEM((rows, width), BF16), table],
        )

    base_shape = jax.ShapeDtypeStruct((tile_rows, width), F32)
    with jax.named_scope("gather_authors"):
        by_z = [shift(author_x, "zh", e) for e in range(1, RING)]
        by_z, tile_one = lax.optimization_barrier((by_z, tile_one))
        own_up, own_down = shift(author_x, "y", 1), shift(author_x, "y", RING - 1)
        by_z, own_up, own_down = lax.optimization_barrier((by_z, own_up, own_down))
        relay = jnp.concatenate(by_z)
        ups, downs = shift(relay, "y", 1), shift(relay, "y", RING - 1)
    base = part(0, 1, [[(0, e)] for e in range(RING)], (author_x, *by_z), None, base_shape)
    with jax.named_scope("forward_authors"):
        ups, downs, base, self_term = lax.optimization_barrier((ups, downs, base, self_term))
        up_two = shift(jnp.concatenate([own_up, ups[:own]]), "y", 1)
        down_two = shift(downs[own:], "y", RING - 1)
    split = [es for g in range(2) for es in ([(g, 0)], [(g, e) for e in range(1, RING)])]
    base = part(1, 2, split, (own_up, ups, own_down, downs), base, base_shape)
    send, msgs = part(
        3,
        1,
        [[(0, 0), (0, 1)], [(0, 2), (0, 3)]],
        (up_two, down_two),
        base,
        shaped(RING, 2),
    )
    keep = call(keep_part, 10**9, (), (msgs, tile_one, base), shaped(RING, 2, dtype=F32), [])
    with jax.named_scope("sum_papers"):
        pair = keep + swap(send, "core").astype(F32)
        by_x = [shift(pair[d].astype(BF16), "x", d) for d in range(1, RING)]
        both = total_of([pair[0], *by_x])
        both = jnp.stack([both[0] + self_term, both[1]])
        both, place = lax.optimization_barrier((both, place))
        got = swap(both.astype(BF16), "zl")
    tile_two = call(
        build_two, 10**9, (place,), (vals,), jax.ShapeDtypeStruct((tile_rows, tile_rows), BF16), []
    )
    got, tile_two = lax.optimization_barrier((got, tile_two))
    paper_hidden, outgoing = call(
        hidden_step, 4 * own * width * width, (), (both, got, w_two), (shaped(), shaped(2)), []
    )
    with jax.named_scope("gather_papers"):
        mine = [outgoing, *(shift(outgoing, "x", d) for d in range(1, RING))]
        other = [swap(m, "core") for m in mine]
    whole = shaped(RING, dtype=F32)
    piece = jax.ShapeDtypeStruct((RING, own // 2, width), BF16)
    two_up, two_down, table = call(
        hop_two_first,
        10**9,
        (),
        (*mine, *other, tile_two),
        (piece, piece, jax.ShapeDtypeStruct((tile_rows, width), BF16)),
        [],
    )
    same, up, down = call(hop_two_rest, 10**9, (), (table, tile_two), (whole, whole, whole), [])
    with jax.named_scope("sum_authors"):
        half = own // 2
        from_down = shift(two_up, "y", 1).astype(F32)
        from_up = shift(two_down, "y", RING - 1).astype(F32)
        up = jnp.concatenate([up[:, :half] + from_down, up[:, half:]], axis=1).astype(BF16)
        down = jnp.concatenate([down[:, :half], down[:, half:] + from_up], axis=1).astype(BF16)
        opposite = total_of([same[0], shift(up[0], "y", 1), shift(down[0], "y", RING - 1)])
        rest = total_of([same[1:], shift(up[1:], "y", 1), shift(down[1:], "y", RING - 1)])
        by_z = [
            shift(opposite.astype(BF16), "zh", 2),
            shift(rest[1].astype(BF16), "zh", 1),
            shift(rest[2].astype(BF16), "zh", RING - 1),
        ]
        author_out = total_of([rest[0], *by_z]).astype(BF16)
    return paper_hidden, author_out


def solution(mesh):
    split = Mesh(mesh.devices.reshape(4, 4, 4, 2, 2), (*PROW, *PCOL))
    tile = P(PROW, PCOL)
    return jax.shard_map(
        per_device,
        mesh=split,
        in_specs=(P((*PROW, *PCOL)), P((*PCOL, *PROW)), P(), P(), P(), tile, tile, tile, tile, tile),
        out_specs=(P((*PROW, *PCOL)), P((*PCOL, *PROW))),
        check_vma=False,
    )
```

```python
import functools

import jax
import jax.numpy as jnp
from jax import lax
from jax.experimental import pallas as pl
from jax.experimental.pallas import tpu as pltpu
from jax.sharding import Mesh
from jax.sharding import PartitionSpec as P

PROW = ("y", "zh")
PCOL = ("x", "zl", "core")
F32 = jnp.float32
BF16 = jnp.bfloat16
VMEM_LIMIT = 24 * 2**20
PLACE = 5
RING = 4


def shift(value, axis, by):
    return lax.ppermute(value, axis, [(i, (i + by) % RING) for i in range(RING)])


def swap(value, axis):
    return lax.ppermute(value, axis, [(0, 1), (1, 0)])


def behind(at, by):
    return lax.rem(at + (RING - by), RING)


def build_one(place, vals, one_ref):
    y, _, x, zl, core = (place[i] for i in range(PLACE))
    slots, side = vals.shape[:2]
    half = side // 2
    span = RING * half
    relations = one_ref.shape[1] // one_ref.shape[0]
    one_ref[...] = jnp.zeros_like(one_ref)

    def slot(k, carry):
        row, col, kind = (place[PLACE + 1 + i * slots + k] for i in range(3))
        d = lax.rem(y + RING - lax.div(col, 2), RING)
        group = jnp.where(d == 2, 3, jnp.where(d == 3, 2, d))
        at = (group * relations + kind) * span + lax.rem(col, 2) * side
        lanes = pl.ds(pl.multiple_of(at, side), side)
        d = lax.rem(lax.div(row, 2) + RING - x, RING)
        e = jnp.where(lax.rem(row, 2) == zl, 0, 1)
        for i, c in enumerate((core, 1 - core)):
            at = (i * RING + d) * side + e * half
            block = vals[k, pl.ds(pl.multiple_of(c * half, half), half), :]
            one_ref[pl.ds(pl.multiple_of(at, half), half), lanes] = block
        return carry

    lax.fori_loop(0, place[PLACE], slot, 0)


def build_two(place, vals, two_ref):
    y, zh, x, zl, core = (place[i] for i in range(PLACE))
    slots, side = vals.shape[:2]
    half = side // 2
    two_ref[...] = jnp.zeros_like(two_ref)

    def slot(k, carry):
        row, col = (place[PLACE + 1 + i * slots + k] for i in range(2))
        block = [vals[k, pl.ds(pl.multiple_of(c * half, half), half), :] for c in (core, 1 - core)]
        turned = jnp.concatenate(block).T
        d = lax.rem(x + RING - lax.div(row, 2), RING)
        e = jnp.where(lax.rem(row, 2) == zl, 0, 1)
        lanes = pl.ds(pl.multiple_of((d * 2 + e) * side, side), side)
        d = lax.rem(lax.div(col, 2) + RING - y, RING)
        for c in range(2):
            e = lax.rem(lax.rem(col, 2) * 2 + c + RING - zh, RING)
            place_of = jnp.where(e == 2, 0, jnp.where(e == 3, 3, e + 1))
            at = (d * RING + place_of) * half
            two_ref[pl.ds(pl.multiple_of(at, half), half), lanes] = turned[c * half : (c + 1) * half]
        return carry

    lax.fori_loop(0, place[PLACE], slot, 0)


def add_product(step, first, tile_ref, msgs_ref, base_ref):
    span = tile_ref.shape[0] // RING
    at = slice(step * span, (step + 1) * span)
    made = jnp.dot(tile_ref[at, first : first + msgs_ref.shape[0]], msgs_ref[...], preferred_element_type=F32)
    return made if base_ref is None else made + base_ref[at, :]


def add_part(first, split, has_base, is_last, place, *refs):
    tile_ref, w_ref, refs = refs[0], refs[1], refs[2:]
    base_ref, refs = (refs[0], refs[1:]) if has_base else (None, refs)
    pieces, (out_ref, msgs, table) = refs[: len(split)], refs[len(split) :]
    relations = w_ref.shape[0]
    span = tile_ref.shape[0] // RING
    own = span // RING
    for piece, chunks in zip(pieces, split, strict=True):
        for i, (group, e) in enumerate(chunks):
            at = pl.multiple_of((group * RING + behind(place[1], e)) * own, own)
            table[pl.ds(at, own), :] = piece[i * own : (i + 1) * own, :]
    for r in range(relations):
        made = jnp.dot(table[...], w_ref[r], preferred_element_type=F32).astype(BF16)
        for i in range(table.shape[0] // span):
            at = (i * relations + r) * span
            msgs[at : at + span, :] = made[i * span : (i + 1) * span]
    skip = first * relations * span
    if is_last:
        for step in range(2):
            made = add_product(2 + step, skip, tile_ref, msgs, base_ref)
            out_ref[2 * step : 2 * step + 2] = made.reshape(2, *out_ref.shape[1:]).astype(BF16)
    else:
        for step in range(RING):
            out_ref[step * span : (step + 1) * span, :] = add_product(step, skip, tile_ref, msgs, base_ref)


def keep_part(msgs_ref, tile_ref, base_ref, out_ref):
    skip = tile_ref.shape[1] - msgs_ref.shape[0]
    for step in range(2):
        made = add_product(step, skip, tile_ref, msgs_ref, base_ref)
        out_ref[2 * step : 2 * step + 2] = made.reshape(2, *out_ref.shape[1:])


def hop_two_first(*refs):
    mine, other, (tile_ref, two_up_ref, two_down_ref, table_ref) = refs[:RING], refs[RING : 2 * RING], refs[2 * RING :]
    own = two_up_ref.shape[1] * 2
    for d in range(RING):
        for e in range(2):
            at = (d * 2 + e) * 2 * own
            table_ref[at : at + own, :] = mine[d][e]
            table_ref[at + own : at + 2 * own, :] = other[d][e]
    span = RING * own
    made = jnp.dot(tile_ref[2 * span : 3 * span, :], table_ref[...], preferred_element_type=F32)
    made = made.astype(BF16).reshape(RING, own, table_ref.shape[1])
    two_up_ref[...] = made[:, : own // 2]
    two_down_ref[...] = made[:, own // 2 :]


def hop_two_rest(table_ref, tile_ref, same_ref, up_ref, down_ref):
    span = same_ref.shape[0] * same_ref.shape[1]
    for d, out in ((1, up_ref), (3, down_ref), (0, same_ref)):
        made = jnp.dot(tile_ref[d * span : (d + 1) * span, :], table_ref[...], preferred_element_type=F32)
        out[...] = made.reshape(out.shape)


def hidden_step(base_ref, got_ref, w_ref, hidden_ref, out_ref):
    first = jnp.maximum(base_ref[0] + got_ref[1].astype(F32), 0.0).astype(BF16)
    second = jnp.maximum(base_ref[1] + got_ref[0].astype(F32), 0.0).astype(BF16)
    hidden_ref[...] = first
    both = jnp.concatenate([first, second])
    out_ref[...] = jnp.dot(both, w_ref[...], preferred_element_type=F32).astype(BF16).reshape(out_ref.shape)


def call(kernel, flops, scalars, arrays, out_shape, scratch):
    def spec(kind):
        return pl.BlockSpec(memory_space=kind)

    return pl.pallas_call(
        kernel,
        out_shape=out_shape,
        in_specs=[spec(pltpu.SMEM)] * len(scalars) + [spec(pltpu.VMEM)] * len(arrays),
        out_specs=jax.tree.map(lambda _: spec(pltpu.VMEM), out_shape),
        scratch_shapes=scratch,
        compiler_params=pltpu.CompilerParams(vmem_limit_bytes=VMEM_LIMIT),
        cost_estimate=pl.CostEstimate(flops=flops, bytes_accessed=4 * 2**20, transcendentals=0),
    )(*scalars, *arrays)


def total_of(parts):
    return sum(p.astype(F32) for p in parts)


def per_device(paper_x, author_x, w_self, w_rel, w_two, block_rows, block_cols, block_type, block_count, block_vals):
    slots = block_rows.shape[2]
    side = block_vals.shape[3]
    own, width = paper_x.shape
    vals = block_vals.reshape(slots, side, side)
    at = jnp.stack([lax.axis_index(a).astype(jnp.int32) for a in (*PROW, *PCOL)])
    place = jnp.concatenate([at, *(a.reshape(-1) for a in (block_count, block_rows, block_cols, block_type))])
    tile_rows = 16 * own

    def shaped(*dims, dtype=BF16):
        return jax.ShapeDtypeStruct((*dims, own, width), dtype)

    relations = w_rel.shape[0]
    tile = jax.ShapeDtypeStruct((tile_rows, relations * tile_rows), BF16)
    tile_one = call(build_one, 10**9, (place,), (vals,), tile, [])
    self_term = jnp.dot(paper_x, w_self, preferred_element_type=F32)
    span = RING * own

    def part(first, groups, split, pieces, base, out_shape):
        is_last = first + groups == RING
        rows = groups * relations * span
        table = pltpu.VMEM((groups * span, width), BF16)
        return call(
            functools.partial(add_part, first, split, base is not None, is_last),
            10**9,
            (place,),
            (tile_one, w_rel, *pieces) if base is None else (tile_one, w_rel, base, *pieces),
            (out_shape, jax.ShapeDtypeStruct((rows, width), BF16)) if is_last else out_shape,
            [table] if is_last else [pltpu.VMEM((rows, width), BF16), table],
        )

    base_shape = jax.ShapeDtypeStruct((tile_rows, width), F32)
    with jax.named_scope("gather_authors"):
        by_z = [shift(author_x, "zh", e) for e in range(1, RING)]
        by_z, tile_one = lax.optimization_barrier((by_z, tile_one))
        own_up, own_down = shift(author_x, "y", 1), shift(author_x, "y", RING - 1)
        by_z, own_up, own_down = lax.optimization_barrier((by_z, own_up, own_down))
        relay = jnp.concatenate(by_z)
        ups, downs = shift(relay, "y", 1), shift(relay, "y", RING - 1)
    base = part(0, 1, [[(0, e)] for e in range(RING)], (author_x, *by_z), None, base_shape)
    split = [[(0, 0)], [(0, e) for e in range(1, RING)]]
    base = part(1, 1, split, (own_up, ups), base, base_shape)
    with jax.named_scope("forward_authors"):
        ups, downs, base, self_term = lax.optimization_barrier((ups, downs, base, self_term))
        up_two = shift(jnp.concatenate([own_up, ups[:own]]), "y", 1)
        down_two = shift(downs[own:], "y", RING - 1)
    base = part(2, 1, split, (own_down, downs), base, base_shape)
    send, msgs = part(
        3,
        1,
        [[(0, 0), (0, 1)], [(0, 2), (0, 3)]],
        (up_two, down_two),
        base,
        shaped(RING, 2),
    )
    keep = call(keep_part, 10**9, (), (msgs, tile_one, base), shaped(RING, 2, dtype=F32), [])
    with jax.named_scope("sum_papers"):
        pair = keep + swap(send, "core").astype(F32)
        by_x = [shift(pair[d].astype(BF16), "x", d) for d in range(1, RING)]
        both = total_of([pair[0], *by_x])
        both = jnp.stack([both[0] + self_term, both[1]])
        both, place = lax.optimization_barrier((both, place))
        got = swap(both.astype(BF16), "zl")
    tile_two = call(
        build_two, 10**9, (place,), (vals,), jax.ShapeDtypeStruct((tile_rows, tile_rows), BF16), []
    )
    got, tile_two = lax.optimization_barrier((got, tile_two))
    paper_hidden, outgoing = call(
        hidden_step, 4 * own * width * width, (), (both, got, w_two), (shaped(), shaped(2)), []
    )
    with jax.named_scope("gather_papers"):
        mine = [outgoing, *(shift(outgoing, "x", d) for d in range(1, RING))]
        other = [swap(m, "core") for m in mine]
    whole = shaped(RING, dtype=F32)
    piece = jax.ShapeDtypeStruct((RING, own // 2, width), BF16)
    two_up, two_down, table = call(
        hop_two_first,
        10**9,
        (),
        (*mine, *other, tile_two),
        (piece, piece, jax.ShapeDtypeStruct((tile_rows, width), BF16)),
        [],
    )
    same, up, down = call(hop_two_rest, 10**9, (), (table, tile_two), (whole, whole, whole), [])
    with jax.named_scope("sum_authors"):
        half = own // 2
        from_down = shift(two_up, "y", 1).astype(F32)
        from_up = shift(two_down, "y", RING - 1).astype(F32)
        up = jnp.concatenate([up[:, :half] + from_down, up[:, half:]], axis=1).astype(BF16)
        down = jnp.concatenate([down[:, :half], down[:, half:] + from_up], axis=1).astype(BF16)
        opposite = total_of([same[0], shift(up[0], "y", 1), shift(down[0], "y", RING - 1)])
        rest = total_of([same[1:], shift(up[1:], "y", 1), shift(down[1:], "y", RING - 1)])
        by_z = [
            shift(opposite.astype(BF16), "zh", 2),
            shift(rest[1].astype(BF16), "zh", 1),
            shift(rest[2].astype(BF16), "zh", RING - 1),
        ]
        author_out = total_of([rest[0], *by_z]).astype(BF16)
    return paper_hidden, author_out


def solution(mesh):
    split = Mesh(mesh.devices.reshape(4, 4, 4, 2, 2), (*PROW, *PCOL))
    tile = P(PROW, PCOL)
    return jax.shard_map(
        per_device,
        mesh=split,
        in_specs=(P((*PROW, *PCOL)), P((*PCOL, *PROW)), P(), P(), P(), tile, tile, tile, tile, tile),
        out_specs=(P((*PROW, *PCOL)), P((*PCOL, *PROW))),
        check_vma=False,
    )
```
